32 devices in a mesh: row: 4 (over z), col: 8 (over y, x, core).
Axes of the slice: x: 2, y: 2, z: 4, core: 2. Of those that a mesh axis runs over, the one named last changes fastest.
Arguments:
- inputs: bfloat16 [768, 8192], P('col', 'row'), may hold values from -6 to 6
- out_grad: bfloat16 [768, 8192], P('col', 'row'), may hold values from -1.5 to 1.5
- w_gate: bfloat16 [8192, 28672], P('row', 'col'), may hold values from -0.0625 to 0.0625
- w_up: bfloat16 [8192, 28672], P('row', 'col'), may hold values from -0.0625 to 0.0625
- w_down: bfloat16 [28672, 8192], P('col', 'row'), may hold values from -0.03125 to 0.03125
Outputs:
- grad_inputs: bfloat16 [768, 8192], P('col', 'row')
- grad_wgate: bfloat16 [8192, 28672], P('row', 'col')
- grad_wup: bfloat16 [8192, 28672], P('row', 'col')
- grad_down: bfloat16 [28672, 8192], P('col', 'row')
The draws below stay inside these ranges and needn't reach their ends.
All inputs are finite; a program needn't handle non-finite values.
Results may differ from the reference program's by a relative error of at most 0.025.
Values may be sent and summed in bfloat16 or wider, within the bound.
A program may use at most 192 MiB of HBM per device.

```python
import jax
import jax.numpy as jnp
from jax import lax

D = 8192
FF = 28672
TOKENS = 768
N_ROW = 4


def shard_levels(key, shape, split, least, top_value):
    loudness = 1.0
    for dim, parts in split:
        draws = jax.random.uniform(jax.random.fold_in(jax.random.fold_in(key, 6), dim), (parts,), jnp.float32, least / len(split), top_value / len(split))
        loudness = loudness * jnp.repeat(jnp.exp(draws), shape[dim] // parts).reshape((-1,) + (1,) * (len(shape) - 1 - dim))
    return loudness


def scatter_about(rng, dims, scale, limit, split=(), dtype=jnp.bfloat16):
    drawn = jax.random.normal(rng, dims, jnp.float32) * scale
    if len(split) > 0:
        drawn = shard_levels(rng, dims, split, -0.22, 0.18) * drawn
    return jnp.clip(drawn, min=-limit, max=limit).astype(dtype)


def setup_inputs(seed: int = 0) -> dict:
    key_of = jax.random.split(jax.random.key(seed), 6)
    return {
        "inputs": scatter_about(key_of[0], (TOKENS, D), 1.0, 6.0, ((0, 8), (1, 4))),
        "out_grad": scatter_about(key_of[1], (TOKENS, D), 0.25, 1.5, ((0, 8), (1, 4))),
        "w_gate": scatter_about(key_of[2], (D, FF), D ** -0.5, 0.0625, ((0, 4), (1, 8))),
        "w_up": scatter_about(key_of[3], (D, FF), D ** -0.5, 0.0625, ((0, 4), (1, 8))),
        "w_down": scatter_about(key_of[4], (FF, D), FF ** -0.5, 0.03125, ((0, 8), (1, 4))),
    }


def rounded(value):
    narrow = lax.optimization_barrier(value.astype(jnp.bfloat16))
    return narrow.astype(jnp.float32)


def reference(inputs, out_grad, w_gate, w_up, w_down):
    block_width = D // N_ROW
    gate = jnp.zeros((TOKENS, FF), jnp.float32)
    up = jnp.zeros((TOKENS, FF), jnp.float32)
    grad_hidden = jnp.zeros((TOKENS, FF), jnp.float32)
    for index_row in range(N_ROW):
        offset = index_row * block_width
        in_block = inputs[:, offset:offset + block_width]
        grad_block = out_grad[:, offset:offset + block_width]
        gate = gate + rounded(jnp.dot(in_block, w_gate[offset:offset + block_width], preferred_element_type=jnp.float32))
        up = up + rounded(jnp.dot(in_block, w_up[offset:offset + block_width], preferred_element_type=jnp.float32))
        grad_hidden = grad_hidden + rounded(lax.dot_general(grad_block, w_down[:, offset:offset + block_width], (((1,), (1,)), ((), ())), preferred_element_type=jnp.float32))
    squash = jax.nn.sigmoid(gate)
    activated = gate * squash
    hidden = (activated * up).astype(jnp.bfloat16)
    grad_gate = (grad_hidden * up * squash * (1.0 + gate * (1.0 - squash))).astype(jnp.bfloat16)
    grad_upact = (grad_hidden * activated).astype(jnp.bfloat16)
    token_contract = (((0,), (0,)), ((), ()))
    grad_down = lax.dot_general(hidden, out_grad, token_contract, preferred_element_type=jnp.float32).astype(jnp.bfloat16)
    grad_wgate = lax.dot_general(inputs, grad_gate, token_contract, preferred_element_type=jnp.float32).astype(jnp.bfloat16)
    grad_wup = lax.dot_general(inputs, grad_upact, token_contract, preferred_element_type=jnp.float32).astype(jnp.bfloat16)
    unit_contract = (((1,), (1,)), ((), ()))
    grad_inputs = lax.dot_general(grad_gate, w_gate, unit_contract, preferred_element_type=jnp.float32)
    grad_inputs = grad_inputs + lax.dot_general(grad_upact, w_up, unit_contract, preferred_element_type=jnp.float32)
    return (grad_inputs.astype(jnp.bfloat16), grad_wgate, grad_wup, grad_down)
```

```python
import functools

import jax
import jax.numpy as jnp
from jax import lax
from jax.experimental import pallas as pl
from jax.experimental.pallas import tpu as pltpu
from jax.sharding import PartitionSpec as P

BF = jnp.bfloat16
F32 = jnp.float32
UNIT = (((1,), (1,)), ((), ()))
TOKEN = (((0,), (0,)), ((), ()))
ANY = pl.BlockSpec(memory_space=pl.ANY)
VMEM_LIMIT = 40 * 1024 * 1024


def divisor(size, *tries):
    for width in tries:
        if size % width == 0:
            return width
    return size


def call(body, grid, in_specs, out_specs, out_shape, cost, aliases=None):
    return pl.pallas_call(
        body,
        grid=grid,
        in_specs=in_specs,
        out_specs=out_specs,
        out_shape=out_shape,
        input_output_aliases=aliases or {},
        cost_estimate=pl.CostEstimate(flops=cost[0], bytes_accessed=cost[1], transcendentals=0),
        compiler_params=pltpu.CompilerParams(vmem_limit_bytes=VMEM_LIMIT),
    )


def first_body(in_ref, grad_ref, wg_ref, wu_ref, wd_ref, *rest):
    out_ref = rest[-1]
    x = in_ref[...]
    out_ref[0] = jnp.dot(x, wg_ref[...], preferred_element_type=F32).astype(BF)
    out_ref[1] = jnp.dot(x, wu_ref[...], preferred_element_type=F32).astype(BF)
    out_ref[2] = lax.dot_general(
        grad_ref[...], wd_ref[...], UNIT, preferred_element_type=F32
    ).astype(BF)


def add_body(mine_ref, got_ref, dep_ref, out_ref):
    out_ref[...] = (mine_ref[...].astype(F32) + got_ref[...].astype(F32)).astype(BF)


def pointwise_body(mine_ref, got_ref, dep_ref, out_ref):
    gate = mine_ref[0].astype(F32) + got_ref[0].astype(F32)
    up = mine_ref[1].astype(F32) + got_ref[1].astype(F32)
    grad_hidden = mine_ref[2].astype(F32) + got_ref[2].astype(F32)
    squash = jax.nn.sigmoid(gate)
    activated = gate * squash
    out_ref[0] = (activated * up).astype(BF)
    out_ref[1] = (grad_hidden * up * squash * (1.0 + gate * (1.0 - squash))).astype(BF)
    out_ref[2] = (grad_hidden * activated).astype(BF)


def select_body(low, high, mine_ref, got_ref, dep_ref, out_ref):
    rank = lax.axis_index("row")
    take = (rank == low) | (rank == high)

    @pl.when(take)
    def _():
        out_ref[...] = got_ref[...]

    @pl.when(jnp.logical_not(take))
    def _():
        out_ref[...] = mine_ref[...]


def second_body(low, high, fresh, *refs):
    mine_ref, got_ref, inT_ref, grad_ref, wg_ref, wu_ref = refs[:6]
    total_in = None if fresh else refs[6]
    total_ref, gw_ref, gu_ref, gd_ref = refs[-4:]
    rank = lax.axis_index("row")
    take = (rank == low) | (rank == high)

    def run(src):
        total = lax.dot_general(src[1], wg_ref[...], UNIT, preferred_element_type=F32)
        total = total + lax.dot_general(src[2], wu_ref[...], UNIT, preferred_element_type=F32)
        total_ref[...] = total if fresh else total_in[...] + total
        gw_ref[...] = jnp.dot(inT_ref[...], src[1], preferred_element_type=F32).astype(BF)
        gu_ref[...] = jnp.dot(inT_ref[...], src[2], preferred_element_type=F32).astype(BF)
        gd_ref[...] = lax.dot_general(
            src[0], grad_ref[...], TOKEN, preferred_element_type=F32
        ).astype(BF)

    @pl.when(take)
    def _():
        run(got_ref)

    @pl.when(jnp.logical_not(take))
    def _():
        run(mine_ref)


def local(n, inputs, out_grad, w_gate, w_up, w_down):
    half = n // 2
    model, units = w_gate.shape
    width = divisor(units, 256, 128)
    count = units // width
    in_all = lax.all_gather(inputs, "col", axis=0, tiled=True)
    grad_all = lax.all_gather(out_grad, "col", axis=0, tiled=True)
    in_T = in_all.T
    tokens = in_all.shape[0]
    rows = divisor(tokens, 384, 256, 128)
    depth = divisor(model, 512, 256, 128)
    pack = jax.ShapeDtypeStruct((3, tokens, width), BF)
    macs = tokens * width * model
    slab = tokens * width * 6

    perms = []
    for s in range(half - 1):
        perms.append([(s, s + 1), (n - 1 - s, n - 2 - s)])
    perms.append([(half - 1, half), (half, half - 1)])
    for s in range(half - 1):
        perms.append([(half - 1 - s, half - 2 - s), (half + s, half + s + 1)])

    def first(k, dep):
        deps = [] if dep is None else [dep]
        return call(
            first_body,
            (tokens // rows,),
            [
                pl.BlockSpec((rows, model), lambda i: (i, 0)),
                pl.BlockSpec((rows, model), lambda i: (i, 0)),
                pl.BlockSpec((model, width), lambda i: (0, k)),
                pl.BlockSpec((model, width), lambda i: (0, k)),
                pl.BlockSpec((width, model), lambda i: (k, 0)),
            ]
            + [ANY] * len(deps),
            pl.BlockSpec((3, rows, width), lambda i: (0, i, 0)),
            pack,
            (6 * macs, tokens * model * 4 + 6 * model * width + slab),
        )(in_all, grad_all, w_gate, w_up, w_down, *deps)

    def combine(j, mine, got, dep):
        if j < half - 1:
            body = add_body
        elif j == half - 1:
            body = pointwise_body
        else:
            s = j - half
            body = functools.partial(select_body, half - 2 - s, half + s + 1)
        spec = pl.BlockSpec((3, rows // 2, width), lambda i: (0, i, 0))
        return call(
            body, (tokens // rows * 2,), [spec, spec, ANY], spec, pack, (10 * slab, 3 * slab)
        )(mine, got, dep)

    def second(k, mine, got, state, dep):
        s = half - 2
        low, high = (half - 2 - s, half + s + 1) if half > 1 else (-1, -1)
        fresh = state is None
        whole = pl.BlockSpec((3, tokens, width), lambda i: (0, 0, 0))
        column = pl.BlockSpec((depth, width), lambda i: (i, k))
        acc = pl.BlockSpec((tokens, depth), lambda i: (0, i))
        ins = [mine, got, in_T, grad_all, w_gate, w_up]
        specs = [whole, whole, pl.BlockSpec((depth, tokens), lambda i: (i, 0)), acc, column, column]
        aliases = {}
        if not fresh:
            ins += list(state)
            specs += [acc, ANY, ANY, ANY]
            aliases = {6: 0, 7: 1, 8: 2, 9: 3}
        ins.append(dep)
        specs.append(ANY)
        return call(
            functools.partial(second_body, low, high, fresh),
            (model // depth,),
            specs,
            [acc, column, column, pl.BlockSpec((width, depth), lambda i: (k, i))],
            [
                jax.ShapeDtypeStruct((tokens, model), F32),
                jax.ShapeDtypeStruct(w_gate.shape, BF),
                jax.ShapeDtypeStruct(w_up.shape, BF),
                jax.ShapeDtypeStruct(w_down.shape, BF),
            ],
            (10 * macs, tokens * model * 12 + 10 * model * width + 2 * slab),
            aliases,
        )(*ins)

    mine, got, state, last = {}, {}, None, None
    for t in range(count + n - 1):
        if t < count:
            last = mine[t] = first(t, last)
            got[t] = lax.ppermute(mine[t], "row", perms[0])
        for j in range(n - 1):
            c = t - 1 - j
            if not 0 <= c < count:
                continue
            if j < n - 2:
                last = mine[c] = combine(j, mine[c], got[c], last)
                got[c] = lax.ppermute(mine[c], "row", perms[j + 1])
            else:
                state = second(c, mine.pop(c), got.pop(c), state, last)
                last = state[3]
    total, gw, gu, gd = state
    grad_inputs = lax.psum_scatter(total.astype(BF), "col", scatter_dimension=0, tiled=True)
    return grad_inputs, gw, gu, gd


def solution(mesh):
    return jax.shard_map(
        functools.partial(local, mesh.shape["row"]),
        mesh=mesh,
        in_specs=(P("col", "row"), P("col", "row"), P("row", "col"), P("row", "col"), P("col", "row")),
        out_specs=(P("col", "row"), P("row", "col"), P("row", "col"), P("col", "row")),
        check_vma=False,
    )
```

```python
import functools

import jax
import jax.numpy as jnp
from jax import lax
from jax.experimental import pallas as pl
from jax.experimental.pallas import tpu as pltpu
from jax.sharding import PartitionSpec as P

BF = jnp.bfloat16
F32 = jnp.float32
UNIT = (((1,), (1,)), ((), ()))
TOKEN = (((0,), (0,)), ((), ()))
ANY = pl.BlockSpec(memory_space=pl.ANY)
VMEM_LIMIT = 40 * 1024 * 1024


def divisor(size, *tries):
    for width in tries:
        if size % width == 0:
            return width
    return size


def call(body, grid, in_specs, out_specs, out_shape, cost, aliases=None):
    return pl.pallas_call(
        body,
        grid=grid,
        in_specs=in_specs,
        out_specs=out_specs,
        out_shape=out_shape,
        input_output_aliases=aliases or {},
        cost_estimate=pl.CostEstimate(flops=cost[0], bytes_accessed=cost[1], transcendentals=0),
        compiler_params=pltpu.CompilerParams(vmem_limit_bytes=VMEM_LIMIT),
    )


def first_body(in_ref, grad_ref, wg_ref, wu_ref, wd_ref, *rest):
    out_ref = rest[-1]
    x = in_ref[...]
    out_ref[0] = jnp.dot(x, wg_ref[...], preferred_element_type=F32).astype(BF)
    out_ref[1] = jnp.dot(x, wu_ref[...], preferred_element_type=F32).astype(BF)
    out_ref[2] = lax.dot_general(
        grad_ref[...], wd_ref[...], UNIT, preferred_element_type=F32
    ).astype(BF)


def add_body(mine_ref, got_ref, dep_ref, out_ref):
    out_ref[...] = (mine_ref[...].astype(F32) + got_ref[...].astype(F32)).astype(BF)


def pointwise_body(mine_ref, got_ref, dep_ref, out_ref):
    gate = mine_ref[0].astype(F32) + got_ref[0].astype(F32)
    up = mine_ref[1].astype(F32) + got_ref[1].astype(F32)
    grad_hidden = mine_ref[2].astype(F32) + got_ref[2].astype(F32)
    squash = jax.nn.sigmoid(gate)
    activated = gate * squash
    out_ref[0] = (activated * up).astype(BF)
    out_ref[1] = (grad_hidden * up * squash * (1.0 + gate * (1.0 - squash))).astype(BF)
    out_ref[2] = (grad_hidden * activated).astype(BF)


def select_body(low, high, mine_ref, got_ref, dep_ref, out_ref):
    rank = lax.axis_index("row")
    take = (rank == low) | (rank == high)

    @pl.when(take)
    def _():
        out_ref[...] = got_ref[...]

    @pl.when(jnp.logical_not(take))
    def _():
        out_ref[...] = mine_ref[...]


def second_body(low, high, fresh, *refs):
    mine_ref, got_ref, inT_ref, grad_ref, wg_ref, wu_ref = refs[:6]
    total_in = None if fresh else refs[6]
    total_ref, gw_ref, gu_ref, gd_ref = refs[-4:]
    rank = lax.axis_index("row")
    take = (rank == low) | (rank == high)

    def run(src):
        total = lax.dot_general(src[1], wg_ref[...], UNIT, preferred_element_type=F32)
        total = total + lax.dot_general(src[2], wu_ref[...], UNIT, preferred_element_type=F32)
        total_ref[...] = total if fresh else total_in[...] + total
        gw_ref[...] = jnp.dot(inT_ref[...], src[1], preferred_element_type=F32).astype(BF)
        gu_ref[...] = jnp.dot(inT_ref[...], src[2], preferred_element_type=F32).astype(BF)
        gd_ref[...] = lax.dot_general(
            src[0], grad_ref[...], TOKEN, preferred_element_type=F32
        ).astype(BF)

    @pl.when(take)
    def _():
        run(got_ref)

    @pl.when(jnp.logical_not(take))
    def _():
        run(mine_ref)


def bits_of(size):
    bits = []
    while 1 << len(bits) < size:
        bits.append(len(bits))
    return bits


def flip(value, size, bit):
    return lax.ppermute(value, "col", [(i, i ^ (1 << bit)) for i in range(size)])


def gather_tokens(size, value, order):
    index = lax.axis_index("col")
    rows, model = value.shape
    current = value
    for bit in order:
        got = flip(current, size, bit)
        upper = ((index >> bit) & 1) == 1
        low = jnp.where(upper, got, current)
        high = jnp.where(upper, current, got)
        current = jnp.stack([low, high])
    held = list(reversed(order))
    axes = [held.index(bit) for bit in sorted(order, reverse=True)]
    current = current.transpose(axes + [len(axes), len(axes) + 1])
    return current.reshape(size * rows, model)


def scatter_tokens(size, value, order):
    index = lax.axis_index("col")
    tokens, model = value.shape
    depth = len(order)
    current = value.reshape((2,) * depth + (tokens // size, model))
    for bit in order:
        axis = depth - 1 - bit
        mine = (index >> bit) & 1
        kept = lax.dynamic_slice_in_dim(current, mine, 1, axis)
        sent = lax.dynamic_slice_in_dim(current, 1 - mine, 1, axis).astype(BF)
        current = kept + flip(sent, size, bit).astype(F32)
    return current.reshape(tokens // size, model).astype(BF)


def local(n, size, inputs, out_grad, w_gate, w_up, w_down):
    half = n // 2
    model, units = w_gate.shape
    width = divisor(units, 256, 128)
    count = units // width
    bits = bits_of(size)
    paired = 1 << len(bits) == size
    up_order = bits[1:] + bits[:1]
    down_order = bits[1:][::-1] + bits[:1]
    if paired:
        in_all = gather_tokens(size, inputs, up_order)
        grad_all = gather_tokens(size, out_grad, down_order)
    else:
        in_all = lax.all_gather(inputs, "col", axis=0, tiled=True)
        grad_all = lax.all_gather(out_grad, "col", axis=0, tiled=True)
    in_T = in_all.T
    tokens = in_all.shape[0]
    rows = divisor(tokens, 384, 256, 128)
    depth = divisor(model, 512, 256, 128)
    pack = jax.ShapeDtypeStruct((3, tokens, width), BF)
    macs = tokens * width * model
    slab = tokens * width * 6

    perms = []
    for s in range(half - 1):
        perms.append([(s, s + 1), (n - 1 - s, n - 2 - s)])
    perms.append([(half - 1, half), (half, half - 1)])
    for s in range(half - 1):
        perms.append([(half - 1 - s, half - 2 - s), (half + s, half + s + 1)])

    def first(k, dep):
        deps = [] if dep is None else [dep]
        return call(
            first_body,
            (tokens // rows,),
            [
                pl.BlockSpec((rows, model), lambda i: (i, 0)),
                pl.BlockSpec((rows, model), lambda i: (i, 0)),
                pl.BlockSpec((model, width), lambda i: (0, k)),
                pl.BlockSpec((model, width), lambda i: (0, k)),
                pl.BlockSpec((width, model), lambda i: (k, 0)),
            ]
            + [ANY] * len(deps),
            pl.BlockSpec((3, rows, width), lambda i: (0, i, 0)),
            pack,
            (6 * macs, tokens * model * 4 + 6 * model * width + slab),
        )(in_all, grad_all, w_gate, w_up, w_down, *deps)

    def combine(j, mine, got, dep):
        if j < half - 1:
            body = add_body
        elif j == half - 1:
            body = pointwise_body
        else:
            s = j - half
            body = functools.partial(select_body, half - 2 - s, half + s + 1)
        spec = pl.BlockSpec((3, rows // 2, width), lambda i: (0, i, 0))
        return call(
            body, (tokens // rows * 2,), [spec, spec, ANY], spec, pack, (10 * slab, 3 * slab)
        )(mine, got, dep)

    def second(k, mine, got, state, dep):
        s = half - 2
        low, high = (half - 2 - s, half + s + 1) if half > 1 else (-1, -1)
        fresh = state is None
        whole = pl.BlockSpec((3, tokens, width), lambda i: (0, 0, 0))
        column = pl.BlockSpec((depth, width), lambda i: (i, k))
        acc = pl.BlockSpec((tokens, depth), lambda i: (0, i))
        ins = [mine, got, in_T, grad_all, w_gate, w_up]
        specs = [whole, whole, pl.BlockSpec((depth, tokens), lambda i: (i, 0)), acc, column, column]
        aliases = {}
        if not fresh:
            ins += list(state)
            specs += [acc, ANY, ANY, ANY]
            aliases = {6: 0, 7: 1, 8: 2, 9: 3}
        if fresh or dep is not state[3]:
            ins.append(dep)
            specs.append(ANY)
        return call(
            functools.partial(second_body, low, high, fresh),
            (model // depth,),
            specs,
            [acc, column, column, pl.BlockSpec((width, depth), lambda i: (k, i))],
            [
                jax.ShapeDtypeStruct((tokens, model), F32),
                jax.ShapeDtypeStruct(w_gate.shape, BF),
                jax.ShapeDtypeStruct(w_up.shape, BF),
                jax.ShapeDtypeStruct(w_down.shape, BF),
            ],
            (10 * macs, tokens * model * 12 + 10 * model * width + 2 * slab),
            aliases,
        )(*ins)

    mine, got, state, last = {}, {}, None, None
    for t in range(count + n - 1):
        if t < count:
            last = mine[t] = first(t, last)
            got[t] = lax.ppermute(mine[t], "row", perms[0])
        for j in range(n - 1):
            c = t - 1 - j
            if not 0 <= c < count:
                continue
            if j < n - 2:
                last = mine[c] = combine(j, mine[c], got[c], last)
                got[c] = lax.ppermute(mine[c], "row", perms[j + 1])
            else:
                state = second(c, mine.pop(c), got.pop(c), state, last)
                last = state[3]
    total, gw, gu, gd = state
    if paired:
        middle = model // 2
        grad_inputs = jnp.concatenate(
            [
                scatter_tokens(size, total[:, :middle], bits),
                scatter_tokens(size, total[:, middle:], bits[:1] + bits[1:][::-1]),
            ],
            axis=1,
        )
    else:
        grad_inputs = lax.psum_scatter(total.astype(BF), "col", scatter_dimension=0, tiled=True)
    return grad_inputs, gw, gu, gd


def solution(mesh):
    return jax.shard_map(
        functools.partial(local, mesh.shape["row"], mesh.shape["col"]),
        mesh=mesh,
        in_specs=(P("col", "row"), P("col", "row"), P("row", "col"), P("row", "col"), P("col", "row")),
        out_specs=(P("col", "row"), P("row", "col"), P("row", "col"), P("col", "row")),
        check_vma=False,
    )
```
